32 devices in a mesh: gx: 2 (over x), yz: 16 (over z, y, core).
Axes of the slice: x: 2, y: 2, z: 4, core: 2. Of those that a mesh axis runs over, the one named last changes fastest.
Arguments:
- old_coeff: bfloat16 [8192, 512], P(('gx', 'yz')), may hold values from -6 to 6
- basis_old: bfloat16 [8, 64, 64], replicated, may hold values from -0.75 to 0.75
- basis_new: bfloat16 [8, 64, 64], replicated, may hold values from -0.75 to 0.75
- quad_weight: float32 [8, 64], replicated, may hold values from 0.3 to 3
- tet_zone: int32 [65536], P(('gx', 'yz')), may hold values from 0 to 255
- tet_table: int32 [65536], P(('gx', 'yz')), may hold values from 0 to 7
- tet_volume: float32 [65536], P(('gx', 'yz')), may hold values from 0.1 to 1
- tet_dest: int32 [65536], P(('gx', 'yz')), may hold values from 0 to 415, as said below
- recv_list: int32 [32, 160], P(('gx', 'yz')), may hold values from 0 to 255
- inv_mass: bfloat16 [8192, 4096], P(('gx', 'yz')), may hold values from -0.75 to 0.75
Outputs:
- new_coeff: float32 [8192, 512], P(('gx', 'yz'))
The draws below stay inside these ranges and needn't reach their ends.
Inputs may be any that keep to these rules, and one draw needn't show every extreme that they name: `tet_dest`: A value below 256 names an own new zone; 256 + k * 16 + s names slot s of partner k.
All inputs are finite; a program needn't handle non-finite values.
Results may differ from the reference program's by a relative error of at most 0.0042.
Values may be sent and summed in bfloat16 or wider, within the bound.
A program may use at most 64 MiB of HBM per device.

```python
import math
import jax
import jax.numpy as jnp
from jax import lax

NB = 64
NF = 8
Q = 64
NTAB = 8
PARTNERS = 10
ZONE_DEV = 256
TET_DEV = 2048
CAP = 16
FACE = 4
ZONES = 8192
TETS = 65536
N_GX = 2
N_YZ = 16
DEVICES = 32


def draw_tet_dest(key, part):
    device_count = TETS // TET_DEV
    keys_all = jax.random.split(key, 5)
    share_draw = jax.random.randint(keys_all[0], (device_count, TET_DEV), 0, 100)
    own_zone = jax.random.randint(keys_all[1], (device_count, TET_DEV), 0, ZONE_DEV)
    far_slot = ZONE_DEV + jax.random.randint(keys_all[2], (device_count, TET_DEV), 0, PARTNERS * CAP)
    dest_value = jnp.where(share_draw < 82, own_zone, far_slot)
    first_place = jax.random.randint(keys_all[3], (device_count, 1), 0, TET_DEV)
    second_place = (first_place + 1 + jax.random.randint(keys_all[4], (device_count, 1), 0, TET_DEV - 1)) % TET_DEV
    column_ids = jnp.arange(TET_DEV, dtype=jnp.int32)[None, :]
    dest_value = jnp.where(column_ids == first_place, ZONE_DEV + PARTNERS * CAP - 1, dest_value)
    dest_value = jnp.where(column_ids == second_place, 0, dest_value)
    return dest_value.reshape(device_count * TET_DEV).astype(jnp.int32)


def place_ends(values, own_key, least, high):
    index_at = [jax.random.randint(jax.random.fold_in(own_key, axis), (), 0, length) for axis, length in enumerate(values.shape)]
    widest = values.shape.index(max(values.shape))
    neighbour = index_at[:widest] + [(index_at[widest] + 1) % values.shape[widest]] + index_at[widest + 1:]
    return values.at[tuple(index_at)].set(least).at[tuple(neighbour)].set(high)


def level_of(own_key, extent, cuts, smallest, top_value):
    gain, own = 1.0, jax.random.fold_in(own_key, 6)
    for axis_at, blocks in cuts:
        draws = jnp.exp(jax.random.uniform(jax.random.fold_in(own, axis_at), (blocks,), jnp.float32, smallest / len(cuts), top_value / len(cuts)))
        gain = gain * jnp.repeat(draws, extent[axis_at] // blocks).reshape([-1 if axis == axis_at else 1 for axis in range(len(extent))])
    return gain


def centred(stream_key, shape, width, bound, cuts=(), held_as=jnp.bfloat16):
    values = width * jax.random.normal(stream_key, shape, jnp.float32)
    if cuts:
        values = values * level_of(stream_key, shape, cuts, -0.22, 0.18)
    return jnp.clip(values, -bound, bound).astype(held_as)


def setup_inputs(seed: int = 0) -> dict:
    key_of = jax.random.split(jax.random.key(seed), 11)
    old_coeff = centred(key_of[0], (ZONES, NB * NF), 1.0, 6.0, ((0, 32),))
    basis_old = centred(key_of[1], (NTAB, Q, NB), NB ** -0.5, 0.75)
    basis_new = centred(key_of[2], (NTAB, Q, NB), Q ** -0.5, 0.75)
    quad_weight = jnp.clip(jnp.exp(jax.random.uniform(key_of[3], (NTAB, Q), jnp.float32, math.log(0.3), math.log(3.0))), 0.3, 3.0)
    tet_zone = place_ends(jax.random.randint(key_of[4], (TETS,), 0, ZONE_DEV), jax.random.fold_in(key_of[4], 1), 0, ZONE_DEV - 1).astype(jnp.int32)
    tet_table = place_ends(jax.random.randint(key_of[5], (TETS,), 0, NTAB), jax.random.fold_in(key_of[5], 1), 0, NTAB - 1).astype(jnp.int32)
    tet_volume = jnp.clip(jnp.exp(math.log(1.0) - 2.3025851 * jax.random.uniform(key_of[6], (TETS,), jnp.float32) ** level_of(key_of[6], (TETS,), ((0, 32),), -0.2, 0.2)), 0.1, 1.0)
    tet_dest = draw_tet_dest(jax.random.fold_in(key_of[10], 71), 0)
    recv_list = place_ends(jax.random.randint(key_of[8], (DEVICES, PARTNERS * CAP), 0, ZONE_DEV), jax.random.fold_in(key_of[8], 1), 0, ZONE_DEV - 1).astype(jnp.int32)
    inv_mass = centred(key_of[9], (ZONES, NB * NB), NB ** -0.5, 0.75, ((0, 32),))
    return {"old_coeff": old_coeff, "basis_old": basis_old, "basis_new": basis_new, "quad_weight": quad_weight, "tet_zone": tet_zone, "tet_table": tet_table, "tet_volume": tet_volume, "tet_dest": tet_dest, "recv_list": recv_list, "inv_mass": inv_mass}


def reference(old_coeff, basis_old, basis_new, quad_weight, tet_zone, tet_table, tet_volume, tet_dest, recv_list, inv_mass):
    row_count = ZONE_DEV + PARTNERS * CAP
    row_width = NB * NF
    coeff_dev = old_coeff.reshape(DEVICES, ZONE_DEV, NB, NF)
    zone_dev = tet_zone.reshape(DEVICES, TET_DEV)
    table_dev = tet_table.reshape(DEVICES, TET_DEV)
    volume_dev = tet_volume.reshape(DEVICES, TET_DEV)
    dest_dev = tet_dest.reshape(DEVICES, TET_DEV)

    def one_device(pieces):
        coeff_one, zone_one, table_one, volume_one, dest_one = pieces
        picked = coeff_one[zone_one].astype(jnp.float32)
        old_rows = basis_old[table_one].astype(jnp.float32)
        values = jnp.einsum("eqi,eif->eqf", old_rows, picked)
        scaling = quad_weight[table_one] * volume_one[:, None]
        weighted = (scaling[:, :, None] * values).astype(jnp.bfloat16)
        new_rows = basis_new[table_one].astype(jnp.float32)
        moment = jnp.einsum("eqj,eqf->ejf", new_rows, weighted.astype(jnp.float32))
        return jax.ops.segment_sum(moment.reshape(TET_DEV, row_width), dest_one, num_segments=row_count)

    partial_value = lax.map(one_device, (coeff_dev, zone_dev, table_dev, volume_dev, dest_dev))
    own_part = partial_value[:, :ZONE_DEV]
    sent = partial_value[:, ZONE_DEV:].astype(jnp.bfloat16).reshape(N_GX, N_YZ, PARTNERS, CAP, row_width)
    offsets = [1, -1, FACE, -FACE, FACE + 1, -FACE - 1, FACE - 1, 1 - FACE]
    arrived = []
    for partner in range(8):
        arrived.append(jnp.roll(sent[:, :, partner], offsets[partner], axis=1))
    arrived.append(jnp.roll(sent[:, :, 8], 1, axis=0))
    arrived.append(jnp.roll(sent[:, :, 9], -1, axis=0))
    received = jnp.stack(arrived, axis=2).reshape(DEVICES, PARTNERS * CAP, row_width)
    inverse_dev = inv_mass.reshape(DEVICES, ZONE_DEV, NB, NB)

    def finish(pieces):
        own_one, received_one, list_one, inverse_one = pieces
        gathered = own_one + jax.ops.segment_sum(received_one.astype(jnp.float32), list_one, num_segments=ZONE_DEV)
        rounded = gathered.astype(jnp.bfloat16).reshape(ZONE_DEV, NB, NF)
        result = jnp.einsum("zjk,zkf->zjf", inverse_one.astype(jnp.float32), rounded.astype(jnp.float32))
        return result.reshape(ZONE_DEV, row_width)

    new_coeff = lax.map(finish, (own_part, received, recv_list, inverse_dev))
    return new_coeff.reshape(DEVICES * ZONE_DEV, row_width)
```

```python
import functools

import jax
import jax.numpy as jnp
from jax import lax
from jax.experimental import pallas as pl
from jax.experimental.pallas import tpu as pltpu
from jax.sharding import PartitionSpec as P

BF = jnp.bfloat16
F32 = jnp.float32
PARTNERS = 10


def nn(left, right):
    return lax.dot_general(left, right, (((1,), (0,)), ((), ())), preferred_element_type=F32)


def nt(left, right):
    return lax.dot_general(left, right, (((1,), (1,)), ((), ())), preferred_element_type=F32)


def halves(value):
    high = value.astype(BF)
    return high, (value - high.astype(F32)).astype(BF)


def iotas(shape):
    return lax.broadcasted_iota(jnp.int32, shape, 0), lax.broadcasted_iota(jnp.int32, shape, 1)


def one_hot(mask):
    return jnp.where(mask, 1.0, 0.0).astype(BF)


def kernel(
    old_ref,
    bold_ref,
    bnew_ref,
    weight_ref,
    zone_ref,
    table_ref,
    volume_ref,
    dest_ref,
    list_ref,
    mass_hbm,
    out_ref,
    mass_ref,
    sent_ref,
    recv_ref,
    perm_ref,
    moved_ref,
    picked_ref,
    dest_hot_ref,
    mass_t_ref,
    gath_t_ref,
    out_t_ref,
    mass_sem,
    send_sem,
    recv_sem,
):
    zones, width = old_ref.shape
    tables, quads, nb = bold_ref.shape
    nf = width // nb
    tets = zone_ref.shape[1]
    slots = list_ref.shape[1]
    cap = slots // PARTNERS
    rows = zones + slots

    mass_copy = pltpu.make_async_copy(mass_hbm, mass_ref, mass_sem)
    mass_copy.start()

    a, b = lax.axis_index("gx"), lax.axis_index("yz")
    n_a, n_b = lax.axis_size("gx"), lax.axis_size("yz")
    face = 1 << (n_b.bit_length() - 1) // 2
    offsets = (1, -1, face, -face, face + 1, -face - 1, face - 1, 1 - face)
    partners = [(a, lax.rem(b + (o + n_b), n_b)) for o in offsets]
    partners += [(lax.rem(a + 1, n_a), b), (lax.rem(a + n_a - 1, n_a), b)]
    barrier = pltpu.get_barrier_semaphore()
    for where in partners:
        pl.semaphore_signal(
            barrier, inc=1, device_id=where, device_id_type=pl.DeviceIdType.MESH
        )

    r, c = iotas((width, width))
    perm_ref[...] = one_hot(r == (c % nb) * nf + c // nb)
    perm = perm_ref[...]

    coeff = nn(old_ref[...], perm).astype(BF)
    quad = 4 * nb
    r, c = iotas((nb, quad))
    bnew4 = nn(bnew_ref[...].reshape(tables * quads, nb), one_hot(r == c % nb)).astype(BF)
    r, c = iotas((nb, nb))
    eye_nb = one_hot(r == c)
    r, c = iotas((quad, quad))
    same = r // nb == c // nb
    for t in range(tables):
        high, low = halves(nt(eye_nb, bold_ref[t]) * weight_ref[t : t + 1, :])
        new_t = bnew4[t * quads : (t + 1) * quads]
        both = nn(high, new_t) + nn(low, new_t)
        block = jnp.where(same, jnp.concatenate([both] * 4, axis=0), 0.0)
        high, low = halves(block)
        for h in range(width // quad):
            part = coeff[:, h * quad : (h + 1) * quad]
            moved_ref[t * zones : (t + 1) * zones, h * quad : (h + 1) * quad] = (
                nn(part, high) + nn(part, low)
            ).astype(BF)

    r, _ = iotas((rows, tets))
    dest_hot_ref[...] = jnp.where(dest_ref[...] == r, volume_ref[...], 0.0).astype(BF)
    r, _ = iotas((zones, tets))
    for t in range(tables):
        of_table = jnp.where(table_ref[...] == t, zone_ref[...], -1)
        picked_ref[:, t * zones : (t + 1) * zones] = nt(
            dest_hot_ref[...], one_hot(of_table == r)
        ).astype(BF)

    sent_ref[...] = nn(picked_ref[zones:, :], moved_ref[...]).astype(BF)
    pl.semaphore_wait(barrier, PARTNERS)
    copies = []
    for k, where in enumerate(partners):
        copy = pltpu.make_async_remote_copy(
            src_ref=sent_ref.at[k * cap : (k + 1) * cap],
            dst_ref=recv_ref.at[k * cap : (k + 1) * cap],
            send_sem=send_sem.at[k],
            recv_sem=recv_sem.at[k],
            device_id=where,
            device_id_type=pl.DeviceIdType.MESH,
        )
        copy.start()
        copies.append(copy)

    own = nn(picked_ref[:zones, :], moved_ref[...])
    mass_copy.wait()
    for o in range(nb // nf):
        mass_t_ref[o * width : (o + 1) * width, :] = nt(
            perm, mass_ref[:, o * width : (o + 1) * width]
        )
    r, _ = iotas((zones, slots))
    list_hot = one_hot(list_ref[...] == r)

    for copy in copies:
        copy.wait()
    gathered = own + nn(list_hot, recv_ref[...])
    gath_t_ref[...] = nt(perm, gathered.astype(BF))

    lanes = 128
    group = 4
    octets = nb // nf
    per_step = 4
    for h in range(zones // lanes):
        at = slice(h * lanes, (h + 1) * lanes)
        for f0 in range(0, nf, group):

            def step(i, sums):
                sums = list(sums)
                for u in range(per_step):
                    base = pl.multiple_of((i * per_step + u) * nf, nf)
                    column = gath_t_ref[pl.ds(base, nf), at]
                    for o in range(octets):
                        mass = mass_t_ref[pl.ds(o * width + base, nf), at]
                        for f in range(group):
                            sums[o * group + f] += mass * column[f0 + f : f0 + f + 1, :]
                return tuple(sums)

            start = tuple(jnp.zeros((nf, lanes), F32) for _ in range(octets * group))
            sums = lax.fori_loop(0, nb // per_step, step, start)
            for o in range(octets):
                for f in range(group):
                    out_t_ref[h, pl.ds(o * nf * nf + f0 + f, nf, stride=nf), :] = sums[
                        o * group + f
                    ]

    r, c = iotas((lanes, lanes))
    eye = one_hot(r == c)
    for h in range(zones // lanes):
        high, low = halves(out_t_ref[h])
        out_ref[h * lanes : (h + 1) * lanes, :] = nt(eye, high) + nt(eye, low)


def on_device(
    old_coeff,
    basis_old,
    basis_new,
    quad_weight,
    tet_zone,
    tet_table,
    tet_volume,
    tet_dest,
    recv_list,
    inv_mass,
):
    zones, width = old_coeff.shape
    tables = basis_old.shape[0]
    nb = basis_old.shape[2]
    tets = tet_zone.shape[0]
    slots = recv_list.shape[1]
    rows = zones + slots
    in_vmem = pl.BlockSpec(memory_space=pltpu.VMEM)
    return pl.pallas_call(
        kernel,
        out_shape=jax.ShapeDtypeStruct((zones, width), F32),
        in_specs=[in_vmem] * 9 + [pl.BlockSpec(memory_space=pl.ANY)],
        out_specs=in_vmem,
        scratch_shapes=[
            pltpu.VMEM(inv_mass.shape, BF),
            pltpu.VMEM((slots, width), BF),
            pltpu.VMEM((slots, width), BF),
            pltpu.VMEM((width, width), BF),
            pltpu.VMEM((tables * zones, width), BF),
            pltpu.VMEM((rows, tables * zones), BF),
            pltpu.VMEM((rows, tets), BF),
            pltpu.VMEM((nb * nb, zones), F32),
            pltpu.VMEM((width, zones), F32),
            pltpu.VMEM((zones // 128, width, 128), F32),
            pltpu.SemaphoreType.DMA,
            pltpu.SemaphoreType.DMA((PARTNERS,)),
            pltpu.SemaphoreType.DMA((PARTNERS,)),
        ],
        compiler_params=pltpu.CompilerParams(
            collective_id=0, has_side_effects=True, vmem_limit_bytes=52 * 2**20
        ),
    )(
        old_coeff,
        basis_old,
        basis_new,
        quad_weight,
        tet_zone.reshape(1, tets),
        tet_table.reshape(1, tets),
        tet_volume.reshape(1, tets),
        tet_dest.reshape(1, tets),
        recv_list,
        inv_mass,
    )


def solution(mesh):
    placed = (
        P(("gx", "yz"), None),
        P(),
        P(),
        P(),
        P(("gx", "yz")),
        P(("gx", "yz")),
        P(("gx", "yz")),
        P(("gx", "yz")),
        P(("gx", "yz"), None),
        P(("gx", "yz"), None),
    )
    return jax.shard_map(
        on_device, mesh=mesh, in_specs=placed, out_specs=P(("gx", "yz"), None), check_vma=False
    )
```

```python
import functools

import jax
import jax.numpy as jnp
from jax import lax
from jax.experimental import pallas as pl
from jax.experimental.pallas import tpu as pltpu
from jax.sharding import PartitionSpec as P

BF = jnp.bfloat16
F32 = jnp.float32
PARTNERS = 10


def nn(left, right):
    return lax.dot_general(left, right, (((1,), (0,)), ((), ())), preferred_element_type=F32)


def nt(left, right):
    return lax.dot_general(left, right, (((1,), (1,)), ((), ())), preferred_element_type=F32)


def halves(value):
    high = value.astype(BF)
    return high, (value - high.astype(F32)).astype(BF)


def iotas(shape):
    return lax.broadcasted_iota(jnp.int32, shape, 0), lax.broadcasted_iota(jnp.int32, shape, 1)


def one_hot(mask):
    return jnp.where(mask, 1.0, 0.0).astype(BF)


def kernel(
    old_hbm,
    bold_hbm,
    bnew_hbm,
    weight_hbm,
    zone_hbm,
    table_hbm,
    volume_hbm,
    dest_hbm,
    list_hbm,
    mass_hbm,
    out_ref,
    old_ref,
    bold_ref,
    bnew_ref,
    weight_ref,
    zone_ref,
    table_ref,
    volume_ref,
    dest_ref,
    list_ref,
    mass_ref,
    sent_ref,
    recv_ref,
    perm_ref,
    moved_ref,
    picked_ref,
    dest_hot_ref,
    mass_t_ref,
    gath_t_ref,
    out_t_ref,
    in_sem,
    send_sem,
    recv_sem,
):
    zones, width = old_ref.shape
    tables, quads, nb = bold_ref.shape
    nf = width // nb
    tets = zone_ref.shape[1]
    slots = list_ref.shape[1]
    cap = slots // PARTNERS
    rows = zones + slots

    pairs = (
        (bnew_hbm, bnew_ref),
        (bold_hbm, bold_ref),
        (weight_hbm, weight_ref),
        (dest_hbm, dest_ref),
        (volume_hbm, volume_ref),
        (zone_hbm, zone_ref),
        (table_hbm, table_ref),
        (old_hbm, old_ref),
        (list_hbm, list_ref),
        (mass_hbm, mass_ref),
    )
    loads = [
        pltpu.make_async_copy(source, target, in_sem.at[i])
        for i, (source, target) in enumerate(pairs)
    ]
    for load in loads:
        load.start()

    a, b = lax.axis_index("gx"), lax.axis_index("yz")
    n_a, n_b = lax.axis_size("gx"), lax.axis_size("yz")
    face = 1 << (n_b.bit_length() - 1) // 2
    offsets = (1, -1, face, -face, face + 1, -face - 1, face - 1, 1 - face)
    partners = [(a, lax.rem(b + (o + n_b), n_b)) for o in offsets]
    partners += [(lax.rem(a + 1, n_a), b), (lax.rem(a + n_a - 1, n_a), b)]
    barrier = pltpu.get_barrier_semaphore()
    for where in partners:
        pl.semaphore_signal(
            barrier, inc=1, device_id=where, device_id_type=pl.DeviceIdType.MESH
        )

    r, c = iotas((width, width))
    perm_ref[...] = one_hot(r == (c % nb) * nf + c // nb)
    perm = perm_ref[...]

    for load in loads[:8]:
        load.wait()
    coeff = nn(old_ref[...], perm).astype(BF)
    quad = 4 * nb
    r, c = iotas((nb, quad))
    bnew4 = nn(bnew_ref[...].reshape(tables * quads, nb), one_hot(r == c % nb)).astype(BF)
    r, c = iotas((nb, nb))
    eye_nb = one_hot(r == c)
    r, c = iotas((quad, quad))
    same = r // nb == c // nb
    for t in range(tables):
        high, low = halves(nt(eye_nb, bold_ref[t]) * weight_ref[t : t + 1, :])
        new_t = bnew4[t * quads : (t + 1) * quads]
        both = nn(high, new_t) + nn(low, new_t)
        block = jnp.where(same, jnp.concatenate([both] * 4, axis=0), 0.0)
        block = block.astype(BF)
        for h in range(width // quad):
            part = coeff[:, h * quad : (h + 1) * quad]
            moved_ref[t * zones : (t + 1) * zones, h * quad : (h + 1) * quad] = nn(
                part, block
            ).astype(BF)

    numbers = iotas((zones, tets))[0].astype(F32).astype(BF)
    one, zero = jnp.ones((), BF), jnp.zeros((), BF)
    volume = volume_ref[...].astype(BF)
    dest = dest_ref[...]
    own_zone = jnp.where(dest < zones, dest, -1).astype(F32).astype(BF)
    far_slot = jnp.where(dest < zones, -1, dest - zones).astype(F32).astype(BF)
    dest_hot_ref[:zones, :] = jnp.where(own_zone == numbers, volume, zero)
    dest_hot_ref[zones:, :] = jnp.where(far_slot == numbers[:slots], volume, zero)
    for t in range(tables):
        of_table = jnp.where(table_ref[...] == t, zone_ref[...], -1).astype(F32).astype(BF)
        picked_ref[:, t * zones : (t + 1) * zones] = nt(
            dest_hot_ref[...], jnp.where(of_table == numbers, one, zero)
        ).astype(BF)

    sent_ref[...] = nn(picked_ref[zones:, :], moved_ref[...]).astype(BF)
    pl.semaphore_wait(barrier, PARTNERS)
    copies = []
    for k, where in enumerate(partners):
        copy = pltpu.make_async_remote_copy(
            src_ref=sent_ref.at[k * cap : (k + 1) * cap],
            dst_ref=recv_ref.at[k * cap : (k + 1) * cap],
            send_sem=send_sem.at[k],
            recv_sem=recv_sem.at[k],
            device_id=where,
            device_id_type=pl.DeviceIdType.MESH,
        )
        copy.start()
        copies.append(copy)

    own = nn(picked_ref[:zones, :], moved_ref[...])
    loads[9].wait()
    for o in range(nb // nf):
        mass_t_ref[o * width : (o + 1) * width, :] = nt(
            perm, mass_ref[:, o * width : (o + 1) * width]
        )
    loads[8].wait()
    r, _ = iotas((zones, slots))
    list_hot = one_hot(list_ref[...] == r)

    for copy in copies:
        copy.wait()
    gathered = own + nn(list_hot, recv_ref[...])
    high, low = halves(gathered)
    gath_t_ref[...] = nt(perm, high) + nt(perm, low)

    lanes = 128
    group = 4
    octets = nb // nf
    per_step = 4
    for h in range(zones // lanes):
        at = slice(h * lanes, (h + 1) * lanes)
        for f0 in range(0, nf, group):

            def step(i, sums):
                sums = list(sums)
                for u in range(per_step):
                    base = pl.multiple_of((i * per_step + u) * nf, nf)
                    column = gath_t_ref[pl.ds(base, nf), at]
                    for o in range(octets):
                        mass = mass_t_ref[pl.ds(o * width + base, nf), at]
                        for f in range(group):
                            sums[o * group + f] += mass * column[f0 + f : f0 + f + 1, :]
                return tuple(sums)

            start = tuple(jnp.zeros((nf, lanes), F32) for _ in range(octets * group))
            sums = lax.fori_loop(0, nb // per_step, step, start)
            for o in range(octets):
                for f in range(group):
                    out_t_ref[h, pl.ds(o * nf * nf + f0 + f, nf, stride=nf), :] = sums[
                        o * group + f
                    ]

    r, c = iotas((lanes, lanes))
    eye = one_hot(r == c)
    for h in range(zones // lanes):
        high, low = halves(out_t_ref[h])
        out_ref[h * lanes : (h + 1) * lanes, :] = nt(eye, high) + nt(eye, low)


def on_device(
    old_coeff,
    basis_old,
    basis_new,
    quad_weight,
    tet_zone,
    tet_table,
    tet_volume,
    tet_dest,
    recv_list,
    inv_mass,
):
    zones, width = old_coeff.shape
    tables = basis_old.shape[0]
    nb = basis_old.shape[2]
    tets = tet_zone.shape[0]
    slots = recv_list.shape[1]
    rows = zones + slots
    operands = (
        old_coeff,
        basis_old,
        basis_new,
        quad_weight,
        tet_zone.reshape(1, tets),
        tet_table.reshape(1, tets),
        tet_volume.reshape(1, tets),
        tet_dest.reshape(1, tets),
        recv_list,
        inv_mass,
    )
    return pl.pallas_call(
        kernel,
        out_shape=jax.ShapeDtypeStruct((zones, width), F32),
        in_specs=[pl.BlockSpec(memory_space=pltpu.HBM)] * len(operands),
        out_specs=pl.BlockSpec(memory_space=pltpu.VMEM),
        scratch_shapes=[
            *(pltpu.VMEM(x.shape, x.dtype) for x in operands),
            pltpu.VMEM((slots, width), BF),
            pltpu.VMEM((slots, width), BF),
            pltpu.VMEM((width, width), BF),
            pltpu.VMEM((tables * zones, width), BF),
            pltpu.VMEM((rows, tables * zones), BF),
            pltpu.VMEM((rows, tets), BF),
            pltpu.VMEM((nb * nb, zones), F32),
            pltpu.VMEM((width, zones), F32),
            pltpu.VMEM((zones // 128, width, 128), F32),
            pltpu.SemaphoreType.DMA((len(operands),)),
            pltpu.SemaphoreType.DMA((PARTNERS,)),
            pltpu.SemaphoreType.DMA((PARTNERS,)),
        ],
        compiler_params=pltpu.CompilerParams(
            collective_id=0, has_side_effects=True, vmem_limit_bytes=62 * 2**20
        ),
    )(*operands)


def solution(mesh):
    placed = (
        P(("gx", "yz"), None),
        P(),
        P(),
        P(),
        P(("gx", "yz")),
        P(("gx", "yz")),
        P(("gx", "yz")),
        P(("gx", "yz")),
        P(("gx", "yz"), None),
        P(("gx", "yz"), None),
    )
    return jax.shard_map(
        on_device, mesh=mesh, in_specs=placed, out_specs=P(("gx", "yz"), None), check_vma=False
    )
```

```python
import functools

import jax
import jax.numpy as jnp
from jax import lax
from jax.experimental import pallas as pl
from jax.experimental.pallas import tpu as pltpu
from jax.sharding import PartitionSpec as P

BF = jnp.bfloat16
F32 = jnp.float32
PARTNERS = 10


def nn(left, right):
    return lax.dot_general(left, right, (((1,), (0,)), ((), ())), preferred_element_type=F32)


def nt(left, right):
    return lax.dot_general(left, right, (((1,), (1,)), ((), ())), preferred_element_type=F32)


def halves(value):
    high = value.astype(BF)
    return high, (value - high.astype(F32)).astype(BF)


def iotas(shape):
    return lax.broadcasted_iota(jnp.int32, shape, 0), lax.broadcasted_iota(jnp.int32, shape, 1)


def one_hot(mask):
    return jnp.where(mask, 1.0, 0.0).astype(BF)


def kernel(
    old_hbm,
    bold_hbm,
    bnew_hbm,
    weight_hbm,
    zone_hbm,
    table_hbm,
    volume_hbm,
    dest_hbm,
    list_hbm,
    mass_hbm,
    out_ref,
    old_ref,
    bold_ref,
    bnew_ref,
    weight_ref,
    zone_ref,
    table_ref,
    volume_ref,
    dest_ref,
    list_ref,
    mass_ref,
    sent_ref,
    recv_ref,
    perm_ref,
    perm_t_ref,
    block_ref,
    moved_ref,
    source_ref,
    own_hot_ref,
    far_ref,
    near_ref,
    mass_t_ref,
    gath_t_ref,
    out_t_ref,
    in_sem,
    send_sem,
    recv_sem,
):
    zones, width = old_ref.shape
    tables, quads, nb = bold_ref.shape
    nf = width // nb
    tets = zone_ref.shape[1]
    slots = list_ref.shape[1]
    cap = slots // PARTNERS

    pairs = (
        (bnew_hbm, bnew_ref),
        (bold_hbm, bold_ref),
        (weight_hbm, weight_ref),
        (dest_hbm, dest_ref),
        (volume_hbm, volume_ref),
        (zone_hbm, zone_ref),
        (table_hbm, table_ref),
        (old_hbm, old_ref),
        (list_hbm, list_ref),
        (mass_hbm, mass_ref),
    )
    loads = [
        pltpu.make_async_copy(source, target, in_sem.at[i])
        for i, (source, target) in enumerate(pairs)
    ]
    for load in loads:
        load.start()

    a, b = lax.axis_index("gx"), lax.axis_index("yz")
    n_a, n_b = lax.axis_size("gx"), lax.axis_size("yz")
    face = 1 << (n_b.bit_length() - 1) // 2
    offsets = (1, -1, face, -face, face + 1, -face - 1, face - 1, 1 - face)
    partners = [(a, lax.rem(b + (o + n_b), n_b)) for o in offsets]
    partners += [(lax.rem(a + 1, n_a), b), (lax.rem(a + n_a - 1, n_a), b)]
    barrier = pltpu.get_barrier_semaphore()
    for where in partners:
        pl.semaphore_signal(
            barrier, inc=1, device_id=where, device_id_type=pl.DeviceIdType.MESH
        )

    r, c = iotas((width, width))
    perm_ref[...] = one_hot(r == (c % nb) * nf + c // nb)
    perm_t_ref[...] = one_hot(c == (r % nb) * nf + r // nb)
    perm = perm_ref[...]

    for load in loads[:8]:
        load.wait()
    coeff = nt(perm_t_ref[...], old_ref[...]).astype(BF)
    quad = 4 * nb
    r, c = iotas((nb, quad))
    bold4 = nn(bold_ref[...].reshape(tables * quads, nb), one_hot(r == c % nb)).astype(BF)
    r, c = iotas((nb, nb))
    eye_nb = one_hot(r == c)
    r, c = iotas((quad, quad))
    same = r // nb == c // nb
    for t in range(tables):
        high, low = halves(nt(eye_nb, bnew_ref[t]) * weight_ref[t : t + 1, :])
        old_t = bold4[t * quads : (t + 1) * quads]
        both = nn(high, old_t) + nn(low, old_t)
        block_ref[t * quad : (t + 1) * quad, :] = jnp.where(
            same, jnp.concatenate([both] * 4, axis=0), 0.0
        ).astype(BF)
    for h in range(width // quad):
        part = nn(block_ref[...], coeff[h * quad : (h + 1) * quad]).astype(BF)
        for t in range(tables):
            moved_ref[h * quad : (h + 1) * quad, t * zones : (t + 1) * zones] = part[
                t * quad : (t + 1) * quad
            ]

    numbers = iotas((zones, tets))[0].astype(F32).astype(BF)
    one, zero = jnp.ones((), BF), jnp.zeros((), BF)
    volume = volume_ref[...].astype(BF)
    dest = dest_ref[...]
    own_zone = jnp.where(dest < zones, dest, -1).astype(F32).astype(BF)
    far_slot = jnp.where(dest < zones, -1, dest - zones).astype(F32).astype(BF)
    far_hot = jnp.where(far_slot == numbers[:slots], volume, zero)
    own_hot_ref[...] = jnp.where(own_zone == numbers, volume, zero)
    chunk = 2
    for t0 in range(0, tables, chunk):
        for t in range(t0, t0 + chunk):
            of_table = jnp.where(table_ref[...] == t, zone_ref[...], -1)
            source_ref[t * zones : (t + 1) * zones, :] = jnp.where(
                of_table.astype(F32).astype(BF) == numbers, one, zero
            )
        at = slice(t0 * zones, (t0 + chunk) * zones)
        far_ref[at, :] = nt(source_ref[at, :], far_hot).astype(BF)

    far_t = nn(moved_ref[...], far_ref[...]).astype(BF)
    r, c = iotas((slots, slots))
    sent_ref[...] = nt(one_hot(r == c), far_t).astype(BF)
    pl.semaphore_wait(barrier, PARTNERS)
    copies = []
    for k, where in enumerate(partners):
        copy = pltpu.make_async_remote_copy(
            src_ref=sent_ref.at[k * cap : (k + 1) * cap],
            dst_ref=recv_ref.at[k * cap : (k + 1) * cap],
            send_sem=send_sem.at[k],
            recv_sem=recv_sem.at[k],
            device_id=where,
            device_id_type=pl.DeviceIdType.MESH,
        )
        copy.start()
        copies.append(copy)

    near_ref[...] = nt(source_ref[...], own_hot_ref[...]).astype(BF)
    gath_t_ref[...] = nn(moved_ref[...], near_ref[...])
    loads[9].wait()
    for o in range(nb // nf):
        mass_t_ref[o * width : (o + 1) * width, :] = nt(
            perm, mass_ref[:, o * width : (o + 1) * width]
        )
    loads[8].wait()
    r, _ = iotas((zones, slots))
    list_hot = one_hot(list_ref[...] == r)

    for copy in copies:
        copy.wait()
    gath_t_ref[...] += lax.dot_general(
        recv_ref[...], list_hot, (((0,), (1,)), ((), ())), preferred_element_type=F32
    )

    lanes = 128
    group = 4
    octets = nb // nf
    for h in range(zones // lanes):
        at = slice(h * lanes, (h + 1) * lanes)
        for f0 in range(0, nf, group):

            def step(i, sums):
                sums = list(sums)
                base = pl.multiple_of(i * nf, nf)
                columns = [
                    gath_t_ref[pl.ds((f0 + f) * nb + base, nf), at] for f in range(group)
                ]
                for u in range(nf):
                    row = pl.multiple_of((i * nf + u) * nf, nf)
                    for o in range(octets):
                        mass = mass_t_ref[pl.ds(o * width + row, nf), at]
                        for f in range(group):
                            sums[o * group + f] += mass * columns[f][u : u + 1, :]
                return tuple(sums)

            start = tuple(jnp.zeros((nf, lanes), F32) for _ in range(octets * group))
            sums = lax.fori_loop(0, nb // nf, step, start)
            for o in range(octets):
                for f in range(group):
                    out_t_ref[h, pl.ds(o * nf * nf + f0 + f, nf, stride=nf), :] = sums[
                        o * group + f
                    ]

    r, c = iotas((lanes, lanes))
    eye = one_hot(r == c)
    for h in range(zones // lanes):
        high, low = halves(out_t_ref[h])
        out_ref[h * lanes : (h + 1) * lanes, :] = nt(eye, high) + nt(eye, low)


def on_device(
    old_coeff,
    basis_old,
    basis_new,
    quad_weight,
    tet_zone,
    tet_table,
    tet_volume,
    tet_dest,
    recv_list,
    inv_mass,
):
    zones, width = old_coeff.shape
    tables = basis_old.shape[0]
    nb = basis_old.shape[2]
    tets = tet_zone.shape[0]
    slots = recv_list.shape[1]
    operands = (
        old_coeff,
        basis_old,
        basis_new,
        quad_weight,
        tet_zone.reshape(1, tets),
        tet_table.reshape(1, tets),
        tet_volume.reshape(1, tets),
        tet_dest.reshape(1, tets),
        recv_list,
        inv_mass,
    )
    return pl.pallas_call(
        kernel,
        out_shape=jax.ShapeDtypeStruct((zones, width), F32),
        in_specs=[pl.BlockSpec(memory_space=pltpu.HBM)] * len(operands),
        out_specs=pl.BlockSpec(memory_space=pltpu.VMEM),
        scratch_shapes=[
            *(pltpu.VMEM(x.shape, x.dtype) for x in operands),
            pltpu.VMEM((slots, width), BF),
            pltpu.VMEM((slots, width), BF),
            pltpu.VMEM((width, width), BF),
            pltpu.VMEM((width, width), BF),
            pltpu.VMEM((tables * 4 * nb, 4 * nb), BF),
            pltpu.VMEM((width, tables * zones), BF),
            pltpu.VMEM((tables * zones, tets), BF),
            pltpu.VMEM((zones, tets), BF),
            pltpu.VMEM((tables * zones, slots), BF),
            pltpu.VMEM((tables * zones, zones), BF),
            pltpu.VMEM((nb * nb, zones), F32),
            pltpu.VMEM((width, zones), F32),
            pltpu.VMEM((zones // 128, width, 128), F32),
            pltpu.SemaphoreType.DMA((len(operands),)),
            pltpu.SemaphoreType.DMA((PARTNERS,)),
            pltpu.SemaphoreType.DMA((PARTNERS,)),
        ],
        compiler_params=pltpu.CompilerParams(
            collective_id=0, has_side_effects=True, vmem_limit_bytes=52 * 2**20
        ),
    )(*(pltpu.with_memory_space_constraint(x, pltpu.HBM) for x in operands))


def solution(mesh):
    placed = (
        P(("gx", "yz"), None),
        P(),
        P(),
        P(),
        P(("gx", "yz")),
        P(("gx", "yz")),
        P(("gx", "yz")),
        P(("gx", "yz")),
        P(("gx", "yz"), None),
        P(("gx", "yz"), None),
    )
    return jax.shard_map(
        on_device, mesh=mesh, in_specs=placed, out_specs=P(("gx", "yz"), None), check_vma=False
    )
```

```python
import functools

import jax
import jax.numpy as jnp
from jax import lax
from jax.experimental import pallas as pl
from jax.experimental.pallas import tpu as pltpu
from jax.sharding import PartitionSpec as P

BF = jnp.bfloat16
F32 = jnp.float32
PARTNERS = 10


def nn(left, right):
    return lax.dot_general(left, right, (((1,), (0,)), ((), ())), preferred_element_type=F32)


def nt(left, right):
    return lax.dot_general(left, right, (((1,), (1,)), ((), ())), preferred_element_type=F32)


def halves(value):
    high = value.astype(BF)
    return high, (value - high.astype(F32)).astype(BF)


def iotas(shape):
    return lax.broadcasted_iota(jnp.int32, shape, 0), lax.broadcasted_iota(jnp.int32, shape, 1)


def one_hot(mask):
    return jnp.where(mask, 1.0, 0.0).astype(BF)


def kernel(
    old_hbm,
    bold_hbm,
    bnew_hbm,
    weight_hbm,
    zone_hbm,
    table_hbm,
    volume_hbm,
    dest_hbm,
    list_hbm,
    mass_hbm,
    out_ref,
    old_ref,
    bold_ref,
    bnew_ref,
    weight_ref,
    zone_ref,
    table_ref,
    volume_ref,
    dest_ref,
    list_ref,
    mass_ref,
    sent_ref,
    recv_ref,
    perm_ref,
    moved_ref,
    zone_hot_ref,
    far_hot_ref,
    own_hot_ref,
    far_ref,
    near_ref,
    mass_t_ref,
    gath_t_ref,
    out_t_ref,
    in_sem,
    send_sem,
    recv_sem,
):
    zones, width = old_ref.shape
    tables, quads, nb = bold_ref.shape
    nf = width // nb
    tets = zone_ref.shape[1]
    slots = list_ref.shape[1]
    cap = slots // PARTNERS

    pairs = (
        (bnew_hbm, bnew_ref),
        (bold_hbm, bold_ref),
        (weight_hbm, weight_ref),
        (dest_hbm, dest_ref),
        (volume_hbm, volume_ref),
        (zone_hbm, zone_ref),
        (table_hbm, table_ref),
        (old_hbm, old_ref),
        (list_hbm, list_ref),
        (mass_hbm, mass_ref),
    )
    loads = [
        pltpu.make_async_copy(source, target, in_sem.at[i])
        for i, (source, target) in enumerate(pairs)
    ]
    for load in loads:
        load.start()

    a, b = lax.axis_index("gx"), lax.axis_index("yz")
    n_a, n_b = lax.axis_size("gx"), lax.axis_size("yz")
    face = 1 << (n_b.bit_length() - 1) // 2
    offsets = (1, -1, face, -face, face + 1, -face - 1, face - 1, 1 - face)
    partners = [(a, lax.rem(b + (o + n_b), n_b)) for o in offsets]
    partners += [(lax.rem(a + 1, n_a), b), (lax.rem(a + n_a - 1, n_a), b)]
    barrier = pltpu.get_barrier_semaphore()
    for where in partners:
        pl.semaphore_signal(
            barrier, inc=1, device_id=where, device_id_type=pl.DeviceIdType.MESH
        )

    r, c = iotas((width, width))
    perm_ref[...] = one_hot(r == (c % nb) * nf + c // nb)
    perm = perm_ref[...]

    for load in loads[:8]:
        load.wait()
    coeff = nn(old_ref[...], perm).astype(BF)
    quad = 4 * nb
    r, c = iotas((nb, quad))
    bnew4 = nn(bnew_ref[...].reshape(tables * quads, nb), one_hot(r == c % nb)).astype(BF)
    r, c = iotas((nb, nb))
    eye_nb = one_hot(r == c)
    r, c = iotas((quad, quad))
    same = r // nb == c // nb
    for t in range(tables):
        high, low = halves(nt(eye_nb, bold_ref[t]) * weight_ref[t : t + 1, :])
        new_t = bnew4[t * quads : (t + 1) * quads]
        both = nn(high, new_t) + nn(low, new_t)
        block = jnp.where(same, jnp.concatenate([both] * 4, axis=0), 0.0)
        block = block.astype(BF)
        for h in range(width // quad):
            part = coeff[:, h * quad : (h + 1) * quad]
            moved_ref[t * zones : (t + 1) * zones, h * quad : (h + 1) * quad] = nn(
                part, block
            ).astype(BF)

    numbers = iotas((zones, tets))[0].astype(F32).astype(BF)
    one, zero = jnp.ones((), BF), jnp.zeros((), BF)
    zone_hot_ref[...] = jnp.where(zone_ref[...].astype(F32).astype(BF) == numbers, one, zero)
    volume = volume_ref[...].astype(BF)

    def spread(target_ref, count, first):
        for t in range(tables):
            wanted = (table_ref[...] == t) & (dest_ref[...] >= first)
            wanted &= dest_ref[...] < first + count
            row = jnp.where(wanted, dest_ref[...] - first, -1).astype(F32).astype(BF)
            target_ref[t * count : (t + 1) * count, :] = jnp.where(
                row == numbers[:count], volume, zero
            )

    def summed(target_ref, sums_ref, count):
        sums = nt(target_ref[...], zone_hot_ref[...]).astype(BF)
        for t in range(tables):
            sums_ref[:, t * zones : (t + 1) * zones] = sums[t * count : (t + 1) * count]
        return nn(sums_ref[...], moved_ref[...])

    spread(far_hot_ref, slots, zones)
    sent_ref[...] = summed(far_hot_ref, far_ref, slots).astype(BF)
    pl.semaphore_wait(barrier, PARTNERS)
    copies = []
    for k, where in enumerate(partners):
        copy = pltpu.make_async_remote_copy(
            src_ref=sent_ref.at[k * cap : (k + 1) * cap],
            dst_ref=recv_ref.at[k * cap : (k + 1) * cap],
            send_sem=send_sem.at[k],
            recv_sem=recv_sem.at[k],
            device_id=where,
            device_id_type=pl.DeviceIdType.MESH,
        )
        copy.start()
        copies.append(copy)

    spread(own_hot_ref, zones, 0)
    own = summed(own_hot_ref, near_ref, zones)
    r, c = iotas((zones, zones))
    eye = one_hot(r == c)
    high, low = halves(own)
    for at in range(0, width, zones):
        part = slice(at, at + zones)
        gath_t_ref[part, :] = nt(eye, high[:, part]) + nt(eye, low[:, part])
    loads[9].wait()
    for at in range(0, nb * nb, zones):
        part = slice(at, at + zones)
        mass_t_ref[part, :] = nt(eye, mass_ref[:, part])
    loads[8].wait()
    r, _ = iotas((zones, slots))
    list_hot = one_hot(list_ref[...] == r)

    for copy in copies:
        copy.wait()
    for at in range(0, width, zones):
        part = slice(at, at + zones)
        recv_t = nt(eye, recv_ref[:, part]).astype(BF)
        gath_t_ref[part, :] += nt(recv_t, list_hot)

    lanes = 128
    group = 4
    octet = 8
    for h in range(zones // lanes):
        at = slice(h * lanes, (h + 1) * lanes)
        for f0 in range(0, nf, group):

            def step(i, carry):
                columns = [
                    [gath_t_ref[pl.ds(f * nb + k, octet), at] for k in range(0, nb, octet)]
                    for f in range(f0, f0 + group)
                ]
                for u in range(octet):
                    j = i * octet + u
                    mass = [
                        mass_t_ref[pl.ds(pl.multiple_of(j * nb + k, octet), octet), at]
                        for k in range(0, nb, octet)
                    ]
                    for f in range(group):
                        terms = [m * g for m, g in zip(mass, columns[f])]
                        while len(terms) > 1:
                            terms = [x + y for x, y in zip(terms[::2], terms[1::2])]
                        out_t_ref[h, pl.ds(j * nf + f0 + f, 1), :] = jnp.sum(
                            terms[0], axis=0, keepdims=True
                        )
                return carry

            lax.fori_loop(0, nb // octet, step, 0)

    r, c = iotas((lanes, lanes))
    eye = one_hot(r == c)
    for h in range(zones // lanes):
        high, low = halves(out_t_ref[h])
        out_ref[h * lanes : (h + 1) * lanes, :] = nt(eye, high) + nt(eye, low)


def on_device(
    old_coeff,
    basis_old,
    basis_new,
    quad_weight,
    tet_zone,
    tet_table,
    tet_volume,
    tet_dest,
    recv_list,
    inv_mass,
):
    zones, width = old_coeff.shape
    tables = basis_old.shape[0]
    nb = basis_old.shape[2]
    tets = tet_zone.shape[0]
    slots = recv_list.shape[1]
    operands = (
        old_coeff,
        basis_old,
        basis_new,
        quad_weight,
        tet_zone.reshape(1, tets),
        tet_table.reshape(1, tets),
        tet_volume.reshape(1, tets),
        tet_dest.reshape(1, tets),
        recv_list,
        inv_mass,
    )
    return pl.pallas_call(
        kernel,
        out_shape=jax.ShapeDtypeStruct((zones, width), F32),
        in_specs=[pl.BlockSpec(memory_space=pltpu.HBM)] * len(operands),
        out_specs=pl.BlockSpec(memory_space=pltpu.VMEM),
        scratch_shapes=[
            *(pltpu.VMEM(x.shape, x.dtype) for x in operands),
            pltpu.VMEM((slots, width), BF),
            pltpu.VMEM((slots, width), BF),
            pltpu.VMEM((width, width), BF),
            pltpu.VMEM((tables * zones, width), BF),
            pltpu.VMEM((zones, tets), BF),
            pltpu.VMEM((tables * slots, tets), BF),
            pltpu.VMEM((tables * zones, tets), BF),
            pltpu.VMEM((slots, tables * zones), BF),
            pltpu.VMEM((zones, tables * zones), BF),
            pltpu.VMEM((nb * nb, zones), F32),
            pltpu.VMEM((width, zones), F32),
            pltpu.VMEM((zones // 128, width, 128), F32),
            pltpu.SemaphoreType.DMA((len(operands),)),
            pltpu.SemaphoreType.DMA((PARTNERS,)),
            pltpu.SemaphoreType.DMA((PARTNERS,)),
        ],
        compiler_params=pltpu.CompilerParams(
            collective_id=0, has_side_effects=True, vmem_limit_bytes=52 * 2**20
        ),
    )(*(pltpu.with_memory_space_constraint(x, pltpu.HBM) for x in operands))


def solution(mesh):
    placed = (
        P(("gx", "yz"), None),
        P(),
        P(),
        P(),
        P(("gx", "yz")),
        P(("gx", "yz")),
        P(("gx", "yz")),
        P(("gx", "yz")),
        P(("gx", "yz"), None),
        P(("gx", "yz"), None),
    )
    return jax.shard_map(
        on_device, mesh=mesh, in_specs=placed, out_specs=P(("gx", "yz"), None), check_vma=False
    )
```

```python
import functools

import jax
import jax.numpy as jnp
from jax import lax
from jax.experimental import pallas as pl
from jax.experimental.pallas import tpu as pltpu
from jax.sharding import PartitionSpec as P

BF = jnp.bfloat16
F32 = jnp.float32
PARTNERS = 10


def nn(left, right):
    return lax.dot_general(left, right, (((1,), (0,)), ((), ())), preferred_element_type=F32)


def nt(left, right):
    return lax.dot_general(left, right, (((1,), (1,)), ((), ())), preferred_element_type=F32)


def halves(value):
    high = value.astype(BF)
    return high, (value - high.astype(F32)).astype(BF)


def iotas(shape):
    return lax.broadcasted_iota(jnp.int32, shape, 0), lax.broadcasted_iota(jnp.int32, shape, 1)


def one_hot(mask):
    return jnp.where(mask, 1.0, 0.0).astype(BF)


def kernel(
    old_hbm,
    bold_hbm,
    bnew_hbm,
    weight_hbm,
    zone_hbm,
    table_hbm,
    volume_hbm,
    dest_hbm,
    list_hbm,
    mass_hbm,
    out_ref,
    old_ref,
    bold_ref,
    bnew_ref,
    weight_ref,
    zone_ref,
    table_ref,
    volume_ref,
    dest_ref,
    list_ref,
    mass_ref,
    sent_ref,
    recv_ref,
    perm_ref,
    moved_ref,
    zone_hot_ref,
    far_hot_ref,
    own_hot_ref,
    far_ref,
    near_ref,
    mass_t_ref,
    gath_t_ref,
    out_t_ref,
    in_sem,
    send_sem,
    recv_sem,
):
    zones, width = old_ref.shape
    tables, quads, nb = bold_ref.shape
    nf = width // nb
    tets = zone_ref.shape[1]
    slots = list_ref.shape[1]
    cap = slots // PARTNERS

    pairs = (
        (zone_hbm, zone_ref),
        (table_hbm, table_ref),
        (dest_hbm, dest_ref),
        (volume_hbm, volume_ref),
        (bnew_hbm, bnew_ref),
        (bold_hbm, bold_ref),
        (weight_hbm, weight_ref),
        (old_hbm, old_ref),
        (list_hbm, list_ref),
        (mass_hbm, mass_ref),
    )
    loads = [
        pltpu.make_async_copy(source, target, in_sem.at[i])
        for i, (source, target) in enumerate(pairs)
    ]
    for load in loads:
        load.start()

    a, b = lax.axis_index("gx"), lax.axis_index("yz")
    n_a, n_b = lax.axis_size("gx"), lax.axis_size("yz")
    face = 1 << (n_b.bit_length() - 1) // 2
    offsets = (1, -1, face, -face, face + 1, -face - 1, face - 1, 1 - face)
    partners = [(a, lax.rem(b + (o + n_b), n_b)) for o in offsets]
    partners += [(lax.rem(a + 1, n_a), b), (lax.rem(a + n_a - 1, n_a), b)]
    barrier = pltpu.get_barrier_semaphore()
    for where in partners:
        pl.semaphore_signal(
            barrier, inc=1, device_id=where, device_id_type=pl.DeviceIdType.MESH
        )

    r, c = iotas((width, width))
    perm_ref[...] = one_hot(r == (c % nb) * nf + c // nb)
    perm = perm_ref[...]

    for load in loads[:4]:
        load.wait()
    numbers = iotas((zones, tets))[0].astype(F32).astype(BF)
    one, zero = jnp.ones((), BF), jnp.zeros((), BF)
    zone_hot_ref[...] = jnp.where(zone_ref[...].astype(F32).astype(BF) == numbers, one, zero)
    volume = volume_ref[...].astype(BF)

    in_table = [
        jnp.where(table_ref[...] == t, 1.0, 0.0).astype(BF) for t in range(tables)
    ]

    def summed(target, hot_ref, sums_ref, chunk):
        count = target.shape[0]
        for t0 in range(0, tables, chunk):
            for t in range(t0, t0 + chunk):
                hot_ref[t * count : (t + 1) * count, :] = target * in_table[t]
            part = hot_ref[t0 * count : (t0 + chunk) * count, :]
            sums = nt(part, zone_hot_ref[...]).astype(BF)
            for t in range(chunk):
                at = (t0 + t) * zones
                sums_ref[:, at : at + zones] = sums[t * count : (t + 1) * count]

    dest = dest_ref[...]
    far_slot = jnp.where(dest < zones, -1, dest - zones).astype(F32).astype(BF)
    summed(jnp.where(far_slot == numbers[:slots], volume, zero), far_hot_ref, far_ref, 4)
    for load in loads[4:8]:
        load.wait()
    coeff = nn(old_ref[...], perm).astype(BF)
    quad = 4 * nb
    r, c = iotas((nb, quad))
    bnew4 = nn(bnew_ref[...].reshape(tables * quads, nb), one_hot(r == c % nb)).astype(BF)
    r, c = iotas((nb, nb))
    eye_nb = one_hot(r == c)
    r, c = iotas((quad, quad))
    same = r // nb == c // nb
    for t in range(tables):
        high, low = halves(nt(eye_nb, bold_ref[t]) * weight_ref[t : t + 1, :])
        new_t = bnew4[t * quads : (t + 1) * quads]
        both = nn(high, new_t) + nn(low, new_t)
        block = jnp.where(same, jnp.concatenate([both] * 4, axis=0), 0.0)
        block = block.astype(BF)
        for h in range(width // quad):
            part = coeff[:, h * quad : (h + 1) * quad]
            moved_ref[t * zones : (t + 1) * zones, h * quad : (h + 1) * quad] = nn(
                part, block
            ).astype(BF)

    sent_ref[...] = nn(far_ref[...], moved_ref[...]).astype(BF)
    pl.semaphore_wait(barrier, PARTNERS)
    copies = []
    for k, where in enumerate(partners):
        copy = pltpu.make_async_remote_copy(
            src_ref=sent_ref.at[k * cap : (k + 1) * cap],
            dst_ref=recv_ref.at[k * cap : (k + 1) * cap],
            send_sem=send_sem.at[k],
            recv_sem=recv_sem.at[k],
            device_id=where,
            device_id_type=pl.DeviceIdType.MESH,
        )
        copy.start()
        copies.append(copy)

    own_zone = jnp.where(dest < zones, dest, -1).astype(F32).astype(BF)
    summed(jnp.where(own_zone == numbers, volume, zero), own_hot_ref, near_ref, 2)
    own = nn(near_ref[...], moved_ref[...])
    r, c = iotas((zones, zones))
    eye = one_hot(r == c)
    high, low = halves(own)
    for at in range(0, width, zones):
        part = slice(at, at + zones)
        gath_t_ref[part, :] = nt(eye, high[:, part]) + nt(eye, low[:, part])
    loads[9].wait()
    for at in range(0, nb * nb, zones):
        part = slice(at, at + zones)
        mass_t_ref[part, :] = nt(eye, mass_ref[:, part])
    loads[8].wait()
    r, _ = iotas((zones, slots))
    list_hot = one_hot(list_ref[...] == r)

    for copy in copies:
        copy.wait()
    for at in range(0, width, zones):
        part = slice(at, at + zones)
        recv_t = nt(eye, recv_ref[:, part]).astype(BF)
        gath_t_ref[part, :] += nt(recv_t, list_hot)

    lanes = 128
    group = 2
    octet = 8
    row, _ = iotas((octet, lanes))

    def folded(sums):
        shift = octet // 2
        while shift:
            first = (row & shift) == 0
            paired = []
            for x, y in zip(sums[:shift], sums[shift:]):
                if shift == octet // 2:
                    other = pltpu.roll(jnp.where(first, y, x), shift, 0)
                    paired.append(jnp.where(first, x, y) + other)
                else:
                    x = x + pltpu.roll(x, octet - shift, 0)
                    y = y + pltpu.roll(y, shift, 0)
                    paired.append(jnp.where(first, x, y))
            sums = paired
            shift //= 2
        return sums[0]

    for h in range(zones // lanes):
        at = slice(h * lanes, (h + 1) * lanes)

        def step(i, carry):
            for f0 in range(0, nf, group):
                columns = [
                    [gath_t_ref[pl.ds(f * nb + k, octet), at] for k in range(0, nb, octet)]
                    for f in range(f0, f0 + group)
                ]
                sums = [[] for _ in range(group)]
                for u in range(octet):
                    base = pl.multiple_of((i * octet + u) * nb, octet)
                    mass = [
                        mass_t_ref[pl.ds(base + k, octet), at] for k in range(0, nb, octet)
                    ]
                    for f in range(group):
                        terms = [m * g for m, g in zip(mass, columns[f])]
                        while len(terms) > 1:
                            terms = [x + y for x, y in zip(terms[::2], terms[1::2])]
                        sums[f].append(terms[0])
                for f in range(group):
                    place = pl.ds(i * octet * nf + f0 + f, octet, stride=nf)
                    out_t_ref[h, place, :] = folded(sums[f])
            return carry

        lax.fori_loop(0, nb // octet, step, 0)

    r, c = iotas((lanes, lanes))
    eye = one_hot(r == c)
    for h in range(zones // lanes):
        high, low = halves(out_t_ref[h])
        out_ref[h * lanes : (h + 1) * lanes, :] = nt(eye, high) + nt(eye, low)


def on_device(
    old_coeff,
    basis_old,
    basis_new,
    quad_weight,
    tet_zone,
    tet_table,
    tet_volume,
    tet_dest,
    recv_list,
    inv_mass,
):
    zones, width = old_coeff.shape
    tables = basis_old.shape[0]
    nb = basis_old.shape[2]
    tets = tet_zone.shape[0]
    slots = recv_list.shape[1]
    operands = (
        old_coeff,
        basis_old,
        basis_new,
        quad_weight,
        tet_zone.reshape(1, tets),
        tet_table.reshape(1, tets),
        tet_volume.reshape(1, tets),
        tet_dest.reshape(1, tets),
        recv_list,
        inv_mass,
    )
    return pl.pallas_call(
        kernel,
        out_shape=jax.ShapeDtypeStruct((zones, width), F32),
        in_specs=[pl.BlockSpec(memory_space=pltpu.HBM)] * len(operands),
        out_specs=pl.BlockSpec(memory_space=pltpu.VMEM),
        scratch_shapes=[
            *(pltpu.VMEM(x.shape, x.dtype) for x in operands),
            pltpu.VMEM((slots, width), BF),
            pltpu.VMEM((slots, width), BF),
            pltpu.VMEM((width, width), BF),
            pltpu.VMEM((tables * zones, width), BF),
            pltpu.VMEM((zones, tets), BF),
            pltpu.VMEM((tables * slots, tets), BF),
            pltpu.VMEM((tables * zones, tets), BF),
            pltpu.VMEM((slots, tables * zones), BF),
            pltpu.VMEM((zones, tables * zones), BF),
            pltpu.VMEM((nb * nb, zones), F32),
            pltpu.VMEM((width, zones), F32),
            pltpu.VMEM((zones // 128, width, 128), F32),
            pltpu.SemaphoreType.DMA((len(operands),)),
            pltpu.SemaphoreType.DMA((PARTNERS,)),
            pltpu.SemaphoreType.DMA((PARTNERS,)),
        ],
        compiler_params=pltpu.CompilerParams(
            collective_id=0, has_side_effects=True, vmem_limit_bytes=52 * 2**20
        ),
    )(*(pltpu.with_memory_space_constraint(x, pltpu.HBM) for x in operands))


def solution(mesh):
    placed = (
        P(("gx", "yz"), None),
        P(),
        P(),
        P(),
        P(("gx", "yz")),
        P(("gx", "yz")),
        P(("gx", "yz")),
        P(("gx", "yz")),
        P(("gx", "yz"), None),
        P(("gx", "yz"), None),
    )
    return jax.shard_map(
        on_device, mesh=mesh, in_specs=placed, out_specs=P(("gx", "yz"), None), check_vma=False
    )
```

```python
import functools

import jax
import jax.numpy as jnp
from jax import lax
from jax.experimental import pallas as pl
from jax.experimental.pallas import tpu as pltpu
from jax.sharding import PartitionSpec as P

BF = jnp.bfloat16
F32 = jnp.float32
PARTNERS = 10


def nn(left, right):
    return lax.dot_general(left, right, (((1,), (0,)), ((), ())), preferred_element_type=F32)


def nt(left, right):
    return lax.dot_general(left, right, (((1,), (1,)), ((), ())), preferred_element_type=F32)


def halves(value):
    high = value.astype(BF)
    return high, (value - high.astype(F32)).astype(BF)


def iotas(shape):
    return lax.broadcasted_iota(jnp.int32, shape, 0), lax.broadcasted_iota(jnp.int32, shape, 1)


def one_hot(mask):
    return jnp.where(mask, 1.0, 0.0).astype(BF)


def kernel(
    old_hbm,
    bold_hbm,
    bnew_hbm,
    weight_hbm,
    zone_hbm,
    table_hbm,
    volume_hbm,
    dest_hbm,
    list_hbm,
    mass_hbm,
    out_ref,
    old_ref,
    bold_ref,
    bnew_ref,
    weight_ref,
    zone_ref,
    table_ref,
    volume_ref,
    dest_ref,
    list_ref,
    mass_ref,
    sent_ref,
    recv_ref,
    perm_ref,
    moved_ref,
    zone_hot_ref,
    far_hot_ref,
    own_hot_ref,
    far_ref,
    near_ref,
    mass_t_ref,
    gath_t_ref,
    out_t_ref,
    in_sem,
    send_sem,
    recv_sem,
):
    zones, width = old_ref.shape
    tables, quads, nb = bold_ref.shape
    nf = width // nb
    tets = zone_ref.shape[1]
    slots = list_ref.shape[1]
    cap = slots // PARTNERS

    pairs = (
        (zone_hbm, zone_ref),
        (table_hbm, table_ref),
        (dest_hbm, dest_ref),
        (volume_hbm, volume_ref),
        (bnew_hbm, bnew_ref),
        (bold_hbm, bold_ref),
        (weight_hbm, weight_ref),
        (old_hbm, old_ref),
        (list_hbm, list_ref),
        (mass_hbm, mass_ref),
    )
    loads = [
        pltpu.make_async_copy(source, target, in_sem.at[i])
        for i, (source, target) in enumerate(pairs)
    ]
    for load in loads[:9]:
        load.start()

    a, b = lax.axis_index("gx"), lax.axis_index("yz")
    n_a, n_b = lax.axis_size("gx"), lax.axis_size("yz")
    face = 1 << (n_b.bit_length() - 1) // 2
    offsets = (1, -1, face, -face, face + 1, -face - 1, face - 1, 1 - face)
    partners = [(a, lax.rem(b + (o + n_b), n_b)) for o in offsets]
    partners += [(lax.rem(a + 1, n_a), b), (lax.rem(a + n_a - 1, n_a), b)]
    barrier = pltpu.get_barrier_semaphore()
    for where in partners:
        pl.semaphore_signal(
            barrier, inc=1, device_id=where, device_id_type=pl.DeviceIdType.MESH
        )

    r, c = iotas((width, width))
    perm_ref[...] = one_hot(r == (c % nb) * nf + c // nb)
    perm = perm_ref[...]

    for load in loads[:8]:
        load.wait()
    loads[9].start()
    coeff = nn(old_ref[...], perm).astype(BF)
    quad = 4 * nb
    r, c = iotas((nb, quad))
    bnew4 = nn(bnew_ref[...].reshape(tables * quads, nb), one_hot(r == c % nb)).astype(BF)
    r, c = iotas((nb, nb))
    eye_nb = one_hot(r == c)
    r, c = iotas((quad, quad))
    same = r // nb == c // nb
    for t in range(tables):
        high, low = halves(nt(eye_nb, bold_ref[t]) * weight_ref[t : t + 1, :])
        new_t = bnew4[t * quads : (t + 1) * quads]
        both = nn(high, new_t) + nn(low, new_t)
        block = jnp.where(same, jnp.concatenate([both] * 4, axis=0), 0.0)
        block = block.astype(BF)
        for h in range(width // quad):
            part = coeff[:, h * quad : (h + 1) * quad]
            moved_ref[t * zones : (t + 1) * zones, h * quad : (h + 1) * quad] = nn(
                part, block
            ).astype(BF)

    numbers = iotas((zones, tets))[0].astype(F32).astype(BF)
    one, zero = jnp.ones((), BF), jnp.zeros((), BF)
    zone_hot_ref[...] = jnp.where(zone_ref[...].astype(F32).astype(BF) == numbers, one, zero)
    volume = volume_ref[...].astype(BF)

    in_table = [
        jnp.where(table_ref[...] == t, 1.0, 0.0).astype(BF) for t in range(tables)
    ]

    def summed(target, hot_ref, sums_ref, chunk):
        count = target.shape[0]
        for t0 in range(0, tables, chunk):
            for t in range(t0, t0 + chunk):
                hot_ref[t * count : (t + 1) * count, :] = target * in_table[t]
            part = hot_ref[t0 * count : (t0 + chunk) * count, :]
            sums = nt(part, zone_hot_ref[...]).astype(BF)
            for t in range(chunk):
                at = (t0 + t) * zones
                sums_ref[:, at : at + zones] = sums[t * count : (t + 1) * count]

    dest = dest_ref[...]
    far_slot = jnp.where(dest < zones, -1, dest - zones).astype(F32).astype(BF)
    summed(jnp.where(far_slot == numbers[:slots], volume, zero), far_hot_ref, far_ref, tables)
    sent_ref[...] = nn(far_ref[...], moved_ref[...]).astype(BF)
    pl.semaphore_wait(barrier, PARTNERS)
    copies = []
    for k, where in enumerate(partners):
        copy = pltpu.make_async_remote_copy(
            src_ref=sent_ref.at[k * cap : (k + 1) * cap],
            dst_ref=recv_ref.at[k * cap : (k + 1) * cap],
            send_sem=send_sem.at[k],
            recv_sem=recv_sem.at[k],
            device_id=where,
            device_id_type=pl.DeviceIdType.MESH,
        )
        copy.start()
        copies.append(copy)

    own_zone = jnp.where(dest < zones, dest, -1).astype(F32).astype(BF)
    summed(jnp.where(own_zone == numbers, volume, zero), own_hot_ref, near_ref, 2)
    own = nn(near_ref[...], moved_ref[...])
    r, c = iotas((zones, zones))
    eye = one_hot(r == c)
    high, low = halves(own)
    for at in range(0, width, zones):
        part = slice(at, at + zones)
        gath_t_ref[part, :] = nt(eye, high[:, part]) + nt(eye, low[:, part])
    loads[9].wait()
    for at in range(0, nb * nb, zones):
        part = slice(at, at + zones)
        mass_t_ref[part, :] = nt(eye, mass_ref[:, part])
    loads[8].wait()
    r, _ = iotas((zones, slots))
    list_hot = one_hot(list_ref[...] == r)

    for copy in copies:
        copy.wait()
    for at in range(0, width, zones):
        part = slice(at, at + zones)
        recv_t = nt(eye, recv_ref[:, part]).astype(BF)
        gath_t_ref[part, :] += nt(recv_t, list_hot)

    lanes = 128
    group = 2
    octet = 8
    row, _ = iotas((octet, lanes))

    def folded(sums):
        shift = octet // 2
        while shift:
            first = (row & shift) == 0
            paired = []
            for x, y in zip(sums[:shift], sums[shift:]):
                if shift == octet // 2:
                    other = pltpu.roll(jnp.where(first, y, x), shift, 0)
                    paired.append(jnp.where(first, x, y) + other)
                else:
                    x = x + pltpu.roll(x, octet - shift, 0)
                    y = y + pltpu.roll(y, shift, 0)
                    paired.append(jnp.where(first, x, y))
            sums = paired
            shift //= 2
        return sums[0]

    for h in range(zones // lanes):
        at = slice(h * lanes, (h + 1) * lanes)

        def step(i, carry):
            for f0 in range(0, nf, group):
                columns = [
                    [gath_t_ref[pl.ds(f * nb + k, octet), at] for k in range(0, nb, octet)]
                    for f in range(f0, f0 + group)
                ]
                sums = [[] for _ in range(group)]
                for u in range(octet):
                    base = pl.multiple_of((i * octet + u) * nb, octet)
                    mass = [
                        mass_t_ref[pl.ds(base + k, octet), at] for k in range(0, nb, octet)
                    ]
                    for f in range(group):
                        terms = [m * g for m, g in zip(mass, columns[f])]
                        while len(terms) > 1:
                            terms = [x + y for x, y in zip(terms[::2], terms[1::2])]
                        sums[f].append(terms[0])
                for f in range(group):
                    place = pl.ds(i * octet * nf + f0 + f, octet, stride=nf)
                    out_t_ref[h, place, :] = folded(sums[f])
            return carry

        lax.fori_loop(0, nb // octet, step, 0)

    r, c = iotas((lanes, lanes))
    eye = one_hot(r == c)
    for h in range(zones // lanes):
        high, low = halves(out_t_ref[h])
        out_ref[h * lanes : (h + 1) * lanes, :] = nt(eye, high) + nt(eye, low)


def on_device(
    old_coeff,
    basis_old,
    basis_new,
    quad_weight,
    tet_zone,
    tet_table,
    tet_volume,
    tet_dest,
    recv_list,
    inv_mass,
):
    zones, width = old_coeff.shape
    tables = basis_old.shape[0]
    nb = basis_old.shape[2]
    tets = tet_zone.shape[0]
    slots = recv_list.shape[1]
    operands = (
        old_coeff,
        basis_old,
        basis_new,
        quad_weight,
        tet_zone.reshape(1, tets),
        tet_table.reshape(1, tets),
        tet_volume.reshape(1, tets),
        tet_dest.reshape(1, tets),
        recv_list,
        inv_mass,
    )
    return pl.pallas_call(
        kernel,
        out_shape=jax.ShapeDtypeStruct((zones, width), F32),
        in_specs=[pl.BlockSpec(memory_space=pltpu.HBM)] * len(operands),
        out_specs=pl.BlockSpec(memory_space=pltpu.VMEM),
        scratch_shapes=[
            *(pltpu.VMEM(x.shape, x.dtype) for x in operands),
            pltpu.VMEM((slots, width), BF),
            pltpu.VMEM((slots, width), BF),
            pltpu.VMEM((width, width), BF),
            pltpu.VMEM((tables * zones, width), BF),
            pltpu.VMEM((zones, tets), BF),
            pltpu.VMEM((tables * slots, tets), BF),
            pltpu.VMEM((tables * zones, tets), BF),
            pltpu.VMEM((slots, tables * zones), BF),
            pltpu.VMEM((zones, tables * zones), BF),
            pltpu.VMEM((nb * nb, zones), F32),
            pltpu.VMEM((width, zones), F32),
            pltpu.VMEM((zones // 128, width, 128), F32),
            pltpu.SemaphoreType.DMA((len(operands),)),
            pltpu.SemaphoreType.DMA((PARTNERS,)),
            pltpu.SemaphoreType.DMA((PARTNERS,)),
        ],
        compiler_params=pltpu.CompilerParams(
            collective_id=0, has_side_effects=True, vmem_limit_bytes=52 * 2**20
        ),
    )(*(pltpu.with_memory_space_constraint(x, pltpu.HBM) for x in operands))


def solution(mesh):
    placed = (
        P(("gx", "yz"), None),
        P(),
        P(),
        P(),
        P(("gx", "yz")),
        P(("gx", "yz")),
        P(("gx", "yz")),
        P(("gx", "yz")),
        P(("gx", "yz"), None),
        P(("gx", "yz"), None),
    )
    return jax.shard_map(
        on_device, mesh=mesh, in_specs=placed, out_specs=P(("gx", "yz"), None), check_vma=False
    )
```

```python
import functools

import jax
import jax.numpy as jnp
from jax import lax
from jax.experimental import pallas as pl
from jax.experimental.pallas import tpu as pltpu
from jax.sharding import PartitionSpec as P

BF = jnp.bfloat16
F32 = jnp.float32
PARTNERS = 10


def nn(left, right):
    return lax.dot_general(left, right, (((1,), (0,)), ((), ())), preferred_element_type=F32)


def nt(left, right):
    return lax.dot_general(left, right, (((1,), (1,)), ((), ())), preferred_element_type=F32)


def halves(value):
    high = value.astype(BF)
    return high, (value - high.astype(F32)).astype(BF)


def iotas(shape):
    return lax.broadcasted_iota(jnp.int32, shape, 0), lax.broadcasted_iota(jnp.int32, shape, 1)


def one_hot(mask):
    return jnp.where(mask, 1.0, 0.0).astype(BF)


def kernel(
    old_hbm,
    bold_hbm,
    bnew_hbm,
    weight_hbm,
    zone_hbm,
    table_hbm,
    volume_hbm,
    dest_hbm,
    list_hbm,
    mass_hbm,
    out_ref,
    old_ref,
    bold_ref,
    bnew_ref,
    weight_ref,
    zone_ref,
    table_ref,
    volume_ref,
    dest_ref,
    list_ref,
    mass_ref,
    sent_ref,
    recv_ref,
    perm_ref,
    moved_ref,
    zone_hot_ref,
    far_hot_ref,
    own_hot_ref,
    far_ref,
    near_ref,
    mass_t_ref,
    gath_t_ref,
    out_t_ref,
    in_sem,
    send_sem,
    recv_sem,
):
    zones, width = old_ref.shape
    tables, quads, nb = bold_ref.shape
    nf = width // nb
    tets = zone_ref.shape[1]
    slots = list_ref.shape[1]
    cap = slots // PARTNERS

    pairs = (
        (bnew_hbm, bnew_ref),
        (bold_hbm, bold_ref),
        (weight_hbm, weight_ref),
        (dest_hbm, dest_ref),
        (volume_hbm, volume_ref),
        (zone_hbm, zone_ref),
        (table_hbm, table_ref),
        (old_hbm, old_ref),
        (list_hbm, list_ref),
        (mass_hbm, mass_ref),
    )
    loads = [
        pltpu.make_async_copy(source, target, in_sem.at[i])
        for i, (source, target) in enumerate(pairs)
    ]
    for load in loads:
        load.start()

    a, b = lax.axis_index("gx"), lax.axis_index("yz")
    n_a, n_b = lax.axis_size("gx"), lax.axis_size("yz")
    face = 1 << (n_b.bit_length() - 1) // 2
    offsets = (1, -1, face, -face, face + 1, -face - 1, face - 1, 1 - face)
    partners = [(a, lax.rem(b + (o + n_b), n_b)) for o in offsets]
    partners += [(lax.rem(a + 1, n_a), b), (lax.rem(a + n_a - 1, n_a), b)]
    barrier = pltpu.get_barrier_semaphore()
    for where in partners:
        pl.semaphore_signal(
            barrier, inc=1, device_id=where, device_id_type=pl.DeviceIdType.MESH
        )

    r, c = iotas((width, width))
    perm_ref[...] = one_hot(r == (c % nb) * nf + c // nb)
    perm = perm_ref[...]

    for load in loads[:8]:
        load.wait()
    coeff = nn(old_ref[...], perm).astype(BF)
    quad = 4 * nb
    r, c = iotas((nb, quad))
    bnew4 = nn(bnew_ref[...].reshape(tables * quads, nb), one_hot(r == c % nb)).astype(BF)
    r, c = iotas((nb, nb))
    eye_nb = one_hot(r == c)
    r, c = iotas((quad, quad))
    same = r // nb == c // nb
    for t in range(tables):
        high, low = halves(nt(eye_nb, bold_ref[t]) * weight_ref[t : t + 1, :])
        new_t = bnew4[t * quads : (t + 1) * quads]
        both = nn(high, new_t) + nn(low, new_t)
        block = jnp.where(same, jnp.concatenate([both] * 4, axis=0), 0.0)
        block = block.astype(BF)
        for h in range(width // quad):
            part = coeff[:, h * quad : (h + 1) * quad]
            moved_ref[t * zones : (t + 1) * zones, h * quad : (h + 1) * quad] = nn(
                part, block
            ).astype(BF)

    numbers = iotas((zones, tets))[0].astype(F32).astype(BF)
    one, zero = jnp.ones((), BF), jnp.zeros((), BF)
    zone_hot_ref[...] = jnp.where(zone_ref[...].astype(F32).astype(BF) == numbers, one, zero)
    volume = volume_ref[...].astype(BF)

    def spread(target_ref, count, first):
        for t in range(tables):
            wanted = (table_ref[...] == t) & (dest_ref[...] >= first)
            wanted &= dest_ref[...] < first + count
            row = jnp.where(wanted, dest_ref[...] - first, -1).astype(F32).astype(BF)
            target_ref[t * count : (t + 1) * count, :] = jnp.where(
                row == numbers[:count], volume, zero
            )

    def summed(target_ref, sums_ref, count):
        sums = nt(target_ref[...], zone_hot_ref[...]).astype(BF)
        for t in range(tables):
            sums_ref[:, t * zones : (t + 1) * zones] = sums[t * count : (t + 1) * count]
        return nn(sums_ref[...], moved_ref[...])

    spread(far_hot_ref, slots, zones)
    sent_ref[...] = summed(far_hot_ref, far_ref, slots).astype(BF)
    pl.semaphore_wait(barrier, PARTNERS)
    copies = []
    for k, where in enumerate(partners):
        copy = pltpu.make_async_remote_copy(
            src_ref=sent_ref.at[k * cap : (k + 1) * cap],
            dst_ref=recv_ref.at[k * cap : (k + 1) * cap],
            send_sem=send_sem.at[k],
            recv_sem=recv_sem.at[k],
            device_id=where,
            device_id_type=pl.DeviceIdType.MESH,
        )
        copy.start()
        copies.append(copy)

    own_zone = jnp.where(dest_ref[...] < zones, dest_ref[...], -1).astype(F32).astype(BF)
    own_hot = jnp.where(own_zone == numbers, volume, zero)
    chunk = 2
    for t0 in range(0, tables, chunk):
        for t in range(t0, t0 + chunk):
            own_hot_ref[t * zones : (t + 1) * zones, :] = own_hot * jnp.where(
                table_ref[...] == t, 1.0, 0.0
            ).astype(BF)
        part = own_hot_ref[t0 * zones : (t0 + chunk) * zones, :]
        sums = nt(part, zone_hot_ref[...]).astype(BF)
        for t in range(chunk):
            at = (t0 + t) * zones
            near_ref[:, at : at + zones] = sums[t * zones : (t + 1) * zones]
    own = nn(near_ref[...], moved_ref[...])
    r, c = iotas((zones, zones))
    eye = one_hot(r == c)
    high, low = halves(own)
    for at in range(0, width, zones):
        part = slice(at, at + zones)
        gath_t_ref[part, :] = nt(eye, high[:, part]) + nt(eye, low[:, part])
    loads[9].wait()
    for at in range(0, nb * nb, zones):
        part = slice(at, at + zones)
        mass_t_ref[part, :] = nt(eye, mass_ref[:, part])
    loads[8].wait()
    r, _ = iotas((zones, slots))
    list_hot = one_hot(list_ref[...] == r)

    for copy in copies:
        copy.wait()
    for at in range(0, width, zones):
        part = slice(at, at + zones)
        recv_t = nt(eye, recv_ref[:, part]).astype(BF)
        gath_t_ref[part, :] += nt(recv_t, list_hot)

    lanes = 128
    group = 2
    octet = 8
    row, _ = iotas((octet, lanes))

    def folded(sums):
        shift = octet // 2
        while shift:
            first = (row & shift) == 0
            paired = []
            for x, y in zip(sums[:shift], sums[shift:]):
                if shift == octet // 2:
                    other = pltpu.roll(jnp.where(first, y, x), shift, 0)
                    paired.append(jnp.where(first, x, y) + other)
                else:
                    x = x + pltpu.roll(x, octet - shift, 0)
                    y = y + pltpu.roll(y, shift, 0)
                    paired.append(jnp.where(first, x, y))
            sums = paired
            shift //= 2
        return sums[0]

    for h in range(zones // lanes):
        at = slice(h * lanes, (h + 1) * lanes)

        def step(i, carry):
            for f0 in range(0, nf, group):
                columns = [
                    [gath_t_ref[pl.ds(f * nb + k, octet), at] for k in range(0, nb, octet)]
                    for f in range(f0, f0 + group)
                ]
                sums = [[] for _ in range(group)]
                for u in range(octet):
                    base = pl.multiple_of((i * octet + u) * nb, octet)
                    mass = [
                        mass_t_ref[pl.ds(base + k, octet), at] for k in range(0, nb, octet)
                    ]
                    for f in range(group):
                        terms = [m * g for m, g in zip(mass, columns[f])]
                        while len(terms) > 1:
                            terms = [x + y for x, y in zip(terms[::2], terms[1::2])]
                        sums[f].append(terms[0])
                for f in range(group):
                    place = pl.ds(i * octet * nf + f0 + f, octet, stride=nf)
                    out_t_ref[h, place, :] = folded(sums[f])
            return carry

        lax.fori_loop(0, nb // octet, step, 0)

    r, c = iotas((lanes, lanes))
    eye = one_hot(r == c)
    for h in range(zones // lanes):
        high, low = halves(out_t_ref[h])
        out_ref[h * lanes : (h + 1) * lanes, :] = nt(eye, high) + nt(eye, low)


def on_device(
    old_coeff,
    basis_old,
    basis_new,
    quad_weight,
    tet_zone,
    tet_table,
    tet_volume,
    tet_dest,
    recv_list,
    inv_mass,
):
    zones, width = old_coeff.shape
    tables = basis_old.shape[0]
    nb = basis_old.shape[2]
    tets = tet_zone.shape[0]
    slots = recv_list.shape[1]
    operands = (
        old_coeff,
        basis_old,
        basis_new,
        quad_weight,
        tet_zone.reshape(1, tets),
        tet_table.reshape(1, tets),
        tet_volume.reshape(1, tets),
        tet_dest.reshape(1, tets),
        recv_list,
        inv_mass,
    )
    return pl.pallas_call(
        kernel,
        out_shape=jax.ShapeDtypeStruct((zones, width), F32),
        in_specs=[pl.BlockSpec(memory_space=pltpu.HBM)] * len(operands),
        out_specs=pl.BlockSpec(memory_space=pltpu.VMEM),
        scratch_shapes=[
            *(pltpu.VMEM(x.shape, x.dtype) for x in operands),
            pltpu.VMEM((slots, width), BF),
            pltpu.VMEM((slots, width), BF),
            pltpu.VMEM((width, width), BF),
            pltpu.VMEM((tables * zones, width), BF),
            pltpu.VMEM((zones, tets), BF),
            pltpu.VMEM((tables * slots, tets), BF),
            pltpu.VMEM((tables * zones, tets), BF),
            pltpu.VMEM((slots, tables * zones), BF),
            pltpu.VMEM((zones, tables * zones), BF),
            pltpu.VMEM((nb * nb, zones), F32),
            pltpu.VMEM((width, zones), F32),
            pltpu.VMEM((zones // 128, width, 128), F32),
            pltpu.SemaphoreType.DMA((len(operands),)),
            pltpu.SemaphoreType.DMA((PARTNERS,)),
            pltpu.SemaphoreType.DMA((PARTNERS,)),
        ],
        compiler_params=pltpu.CompilerParams(
            collective_id=0, has_side_effects=True, vmem_limit_bytes=52 * 2**20
        ),
    )(*(pltpu.with_memory_space_constraint(x, pltpu.HBM) for x in operands))


def solution(mesh):
    placed = (
        P(("gx", "yz"), None),
        P(),
        P(),
        P(),
        P(("gx", "yz")),
        P(("gx", "yz")),
        P(("gx", "yz")),
        P(("gx", "yz")),
        P(("gx", "yz"), None),
        P(("gx", "yz"), None),
    )
    return jax.shard_map(
        on_device, mesh=mesh, in_specs=placed, out_specs=P(("gx", "yz"), None), check_vma=False
    )
```

```python
import functools

import jax
import jax.numpy as jnp
from jax import lax
from jax.experimental import pallas as pl
from jax.experimental.pallas import tpu as pltpu
from jax.sharding import PartitionSpec as P

BF = jnp.bfloat16
F32 = jnp.float32
PARTNERS = 10


def nn(left, right):
    return lax.dot_general(left, right, (((1,), (0,)), ((), ())), preferred_element_type=F32)


def nt(left, right):
    return lax.dot_general(left, right, (((1,), (1,)), ((), ())), preferred_element_type=F32)


def halves(value):
    high = value.astype(BF)
    return high, (value - high.astype(F32)).astype(BF)


def iotas(shape):
    return lax.broadcasted_iota(jnp.int32, shape, 0), lax.broadcasted_iota(jnp.int32, shape, 1)


def one_hot(mask):
    return jnp.where(mask, 1.0, 0.0).astype(BF)


def kernel(
    old_hbm,
    bold_hbm,
    bnew_hbm,
    weight_hbm,
    zone_hbm,
    table_hbm,
    volume_hbm,
    dest_hbm,
    list_hbm,
    mass_hbm,
    out_ref,
    old_ref,
    bold_ref,
    bnew_ref,
    weight_ref,
    zone_ref,
    table_ref,
    volume_ref,
    dest_ref,
    list_ref,
    mass_ref,
    sent_ref,
    recv_ref,
    perm_ref,
    moved_ref,
    zone_hot_ref,
    far_hot_ref,
    own_hot_ref,
    far_ref,
    near_ref,
    mass_t_ref,
    gath_t_ref,
    out_t_ref,
    in_sem,
    send_sem,
    recv_sem,
):
    zones, width = old_ref.shape
    tables, quads, nb = bold_ref.shape
    nf = width // nb
    tets = zone_ref.shape[1]
    slots = list_ref.shape[1]
    cap = slots // PARTNERS

    pairs = (
        (bnew_hbm, bnew_ref),
        (bold_hbm, bold_ref),
        (weight_hbm, weight_ref),
        (dest_hbm, dest_ref),
        (volume_hbm, volume_ref),
        (zone_hbm, zone_ref),
        (table_hbm, table_ref),
        (old_hbm, old_ref),
        (list_hbm, list_ref),
        (mass_hbm, mass_ref),
    )
    loads = [
        pltpu.make_async_copy(source, target, in_sem.at[i])
        for i, (source, target) in enumerate(pairs)
    ]
    for load in loads:
        load.start()

    a, b = lax.axis_index("gx"), lax.axis_index("yz")
    n_a, n_b = lax.axis_size("gx"), lax.axis_size("yz")
    face = 1 << (n_b.bit_length() - 1) // 2
    offsets = (1, -1, face, -face, face + 1, -face - 1, face - 1, 1 - face)
    partners = [(a, lax.rem(b + (o + n_b), n_b)) for o in offsets]
    partners += [(lax.rem(a + 1, n_a), b), (lax.rem(a + n_a - 1, n_a), b)]
    barrier = pltpu.get_barrier_semaphore()
    for where in partners:
        pl.semaphore_signal(
            barrier, inc=1, device_id=where, device_id_type=pl.DeviceIdType.MESH
        )

    r, c = iotas((width, width))
    perm_ref[...] = one_hot(r == (c % nb) * nf + c // nb)
    perm = perm_ref[...]

    for load in loads[:8]:
        load.wait()
    coeff = nn(old_ref[...], perm).astype(BF)
    quad = 4 * nb
    r, c = iotas((nb, quad))
    bnew4 = nn(bnew_ref[...].reshape(tables * quads, nb), one_hot(r == c % nb)).astype(BF)
    r, c = iotas((nb, nb))
    eye_nb = one_hot(r == c)
    r, c = iotas((quad, quad))
    same = r // nb == c // nb
    for t in range(tables):
        high, low = halves(nt(eye_nb, bold_ref[t]) * weight_ref[t : t + 1, :])
        new_t = bnew4[t * quads : (t + 1) * quads]
        both = nn(high, new_t) + nn(low, new_t)
        block = jnp.where(same, jnp.concatenate([both] * 4, axis=0), 0.0)
        block = block.astype(BF)
        for h in range(width // quad):
            part = coeff[:, h * quad : (h + 1) * quad]
            moved_ref[t * zones : (t + 1) * zones, h * quad : (h + 1) * quad] = nn(
                part, block
            ).astype(BF)

    numbers = iotas((zones, tets))[0].astype(F32).astype(BF)
    one, zero = jnp.ones((), BF), jnp.zeros((), BF)
    zone_hot_ref[...] = jnp.where(zone_ref[...].astype(F32).astype(BF) == numbers, one, zero)
    volume = volume_ref[...].astype(BF)

    def spread(target_ref, count, first):
        for t in range(tables):
            wanted = (table_ref[...] == t) & (dest_ref[...] >= first)
            wanted &= dest_ref[...] < first + count
            row = jnp.where(wanted, dest_ref[...] - first, -1).astype(F32).astype(BF)
            target_ref[t * count : (t + 1) * count, :] = jnp.where(
                row == numbers[:count], volume, zero
            )

    def summed(target_ref, sums_ref, count):
        sums = nt(target_ref[...], zone_hot_ref[...]).astype(BF)
        for t in range(tables):
            sums_ref[:, t * zones : (t + 1) * zones] = sums[t * count : (t + 1) * count]
        return nn(sums_ref[...], moved_ref[...])

    spread(far_hot_ref, slots, zones)
    sent_ref[...] = summed(far_hot_ref, far_ref, slots).astype(BF)
    pl.semaphore_wait(barrier, PARTNERS)
    copies = []
    for k, where in enumerate(partners):
        copy = pltpu.make_async_remote_copy(
            src_ref=sent_ref.at[k * cap : (k + 1) * cap],
            dst_ref=recv_ref.at[k * cap : (k + 1) * cap],
            send_sem=send_sem.at[k],
            recv_sem=recv_sem.at[k],
            device_id=where,
            device_id_type=pl.DeviceIdType.MESH,
        )
        copy.start()
        copies.append(copy)

    own_zone = jnp.where(dest_ref[...] < zones, dest_ref[...], -1).astype(F32).astype(BF)
    own_hot = jnp.where(own_zone == numbers, volume, zero)
    chunk = 2
    for t0 in range(0, tables, chunk):
        for t in range(t0, t0 + chunk):
            own_hot_ref[t * zones : (t + 1) * zones, :] = own_hot * jnp.where(
                table_ref[...] == t, 1.0, 0.0
            ).astype(BF)
        part = own_hot_ref[t0 * zones : (t0 + chunk) * zones, :]
        sums = nt(part, zone_hot_ref[...]).astype(BF)
        for t in range(chunk):
            at = (t0 + t) * zones
            near_ref[:, at : at + zones] = sums[t * zones : (t + 1) * zones]
    own = nn(near_ref[...], moved_ref[...])
    high, low = halves(own)
    gath_t_ref[...] = nt(perm, high) + nt(perm, low)
    loads[9].wait()
    for o in range(nb // nf):
        mass_t_ref[o * width : (o + 1) * width, :] = nt(
            perm, mass_ref[:, o * width : (o + 1) * width]
        )
    loads[8].wait()
    r, _ = iotas((zones, slots))
    list_hot = one_hot(list_ref[...] == r)

    for copy in copies:
        copy.wait()
    recv_t = nt(perm, recv_ref[...]).astype(BF)
    gath_t_ref[...] += nt(recv_t, list_hot)

    lanes = 128
    group = 4
    octets = nb // nf
    per_step = 4
    for h in range(zones // lanes):
        at = slice(h * lanes, (h + 1) * lanes)
        for f0 in range(0, nf, group):

            def step(i, sums):
                sums = list(sums)
                for u in range(per_step):
                    base = pl.multiple_of((i * per_step + u) * nf, nf)
                    column = gath_t_ref[pl.ds(base, nf), at]
                    for o in range(octets):
                        mass = mass_t_ref[pl.ds(o * width + base, nf), at]
                        for f in range(group):
                            sums[o * group + f] += mass * column[f0 + f : f0 + f + 1, :]
                return tuple(sums)

            start = tuple(jnp.zeros((nf, lanes), F32) for _ in range(octets * group))
            sums = lax.fori_loop(0, nb // per_step, step, start)
            for o in range(octets):
                for f in range(group):
                    out_t_ref[h, pl.ds(o * nf * nf + f0 + f, nf, stride=nf), :] = sums[
                        o * group + f
                    ]

    r, c = iotas((lanes, lanes))
    eye = one_hot(r == c)
    for h in range(zones // lanes):
        high, low = halves(out_t_ref[h])
        out_ref[h * lanes : (h + 1) * lanes, :] = nt(eye, high) + nt(eye, low)


def on_device(
    old_coeff,
    basis_old,
    basis_new,
    quad_weight,
    tet_zone,
    tet_table,
    tet_volume,
    tet_dest,
    recv_list,
    inv_mass,
):
    zones, width = old_coeff.shape
    tables = basis_old.shape[0]
    nb = basis_old.shape[2]
    tets = tet_zone.shape[0]
    slots = recv_list.shape[1]
    operands = (
        old_coeff,
        basis_old,
        basis_new,
        quad_weight,
        tet_zone.reshape(1, tets),
        tet_table.reshape(1, tets),
        tet_volume.reshape(1, tets),
        tet_dest.reshape(1, tets),
        recv_list,
        inv_mass,
    )
    return pl.pallas_call(
        kernel,
        out_shape=jax.ShapeDtypeStruct((zones, width), F32),
        in_specs=[pl.BlockSpec(memory_space=pltpu.HBM)] * len(operands),
        out_specs=pl.BlockSpec(memory_space=pltpu.VMEM),
        scratch_shapes=[
            *(pltpu.VMEM(x.shape, x.dtype) for x in operands),
            pltpu.VMEM((slots, width), BF),
            pltpu.VMEM((slots, width), BF),
            pltpu.VMEM((width, width), BF),
            pltpu.VMEM((tables * zones, width), BF),
            pltpu.VMEM((zones, tets), BF),
            pltpu.VMEM((tables * slots, tets), BF),
            pltpu.VMEM((tables * zones, tets), BF),
            pltpu.VMEM((slots, tables * zones), BF),
            pltpu.VMEM((zones, tables * zones), BF),
            pltpu.VMEM((nb * nb, zones), F32),
            pltpu.VMEM((width, zones), F32),
            pltpu.VMEM((zones // 128, width, 128), F32),
            pltpu.SemaphoreType.DMA((len(operands),)),
            pltpu.SemaphoreType.DMA((PARTNERS,)),
            pltpu.SemaphoreType.DMA((PARTNERS,)),
        ],
        compiler_params=pltpu.CompilerParams(
            collective_id=0, has_side_effects=True, vmem_limit_bytes=52 * 2**20
        ),
    )(*(pltpu.with_memory_space_constraint(x, pltpu.HBM) for x in operands))


def solution(mesh):
    placed = (
        P(("gx", "yz"), None),
        P(),
        P(),
        P(),
        P(("gx", "yz")),
        P(("gx", "yz")),
        P(("gx", "yz")),
        P(("gx", "yz")),
        P(("gx", "yz"), None),
        P(("gx", "yz"), None),
    )
    return jax.shard_map(
        on_device, mesh=mesh, in_specs=placed, out_specs=P(("gx", "yz"), None), check_vma=False
    )
```
